128 devices in a mesh: row: 16 (over y, x_hi, core), col: 8 (over z, x_lo).
Axes of the slice: x: 4 (x_hi: 2, x_lo: 2; x = x_hi * 2 + x_lo), y: 4, z: 4, core: 2. Of those that a mesh axis runs over, the one named last changes fastest.
Arguments:
- a_blocks: bfloat16 [128, 256, 128, 128], P('row', 'col'), may hold values from -6 to 6
- a_pattern: int32 [128, 256], P('row', 'col'), may hold values from 0 to 1, as said below
- b_blocks: bfloat16 [256, 128, 128, 128], P('row', 'col'), may hold values from -0.5 to 0.5
- b_pattern: int32 [256, 128], P('row', 'col'), may hold values from 0 to 1, as said below
Outputs:
- c_blocks: float32 [128, 128, 128, 128], P('row', 'col')
The draws below stay inside these ranges and needn't reach their ends.
Inputs may be any that keep to these rules, and one draw needn't show every extreme that they name: `a_pattern`: each tile of 8 x 16 entries holds at most 16 ones, and in every tile row one tile holds exactly 16. `b_pattern`: each tile of 16 x 8 entries holds at most 16 ones, and in every tile row one tile holds exactly 16.
All inputs are finite; a program needn't handle non-finite values.
Results may differ from the reference program's by a relative error of at most 0.0003.
Values may be sent and summed in bfloat16 or wider, within the bound.
No kernel may reach another device: no remote copies, remote signals or barrier semaphores. Data moves between devices by JAX's collectives and lax.ppermute only.
A program may use at most 128 MiB of HBM per device.

```python
import jax
import jax.numpy as jnp
from jax import lax

BLOCK = 128
BR = 8
KS = 16
BC = 8
CAP_A = 16
CAP_B = 16
A_ROWS = 128
A_COLS = 256
B_ROWS = 256
B_COLS = 128
N_ROW = 16


def tile_pattern(key, tile_rows, tile_cols, rows, cols, capacity):
    key_heavy, key_light, key_score = jax.random.split(key, 3)
    heavy = jax.random.randint(key_heavy, (tile_rows,), 0, tile_cols)
    light = jax.random.randint(key_light, (tile_rows, tile_cols), max(capacity // 4, 1), capacity // 2 + 1)
    counts = jnp.where(jnp.arange(tile_cols)[None, :] == heavy[:, None], capacity, light)
    places = rows * cols
    scores = jax.random.randint(key_score, (tile_rows, tile_cols, places), 0, 1 << 20) * places + jnp.arange(places)[None, None, :]
    ranks = jnp.argsort(jnp.argsort(scores, axis=-1), axis=-1)
    present = (ranks < counts[:, :, None]).astype(jnp.int32)
    present = present.reshape(tile_rows, tile_cols, rows, cols).transpose(0, 2, 1, 3)
    return present.reshape(tile_rows * rows, tile_cols * cols)


def draw_a_pattern(key, part):
    key = jax.random.fold_in(key, 11)
    return tile_pattern(key, N_ROW, N_ROW, BR, KS, CAP_A)


def draw_b_pattern(key, part):
    key = jax.random.fold_in(key, 23)
    return tile_pattern(key, N_ROW, N_ROW, KS, BC, CAP_B)


def levels(rng, dims, shards, smallest, top_value):
    gain, own = 1.0, jax.random.fold_in(rng, 6)
    for dim, shards_of in shards:
        heights = jnp.exp(jax.random.uniform(jax.random.fold_in(own, dim), (shards_of,), jnp.float32, smallest / len(shards), top_value / len(shards)))
        gain = gain * jnp.repeat(heights, dims[dim] // shards_of).reshape([-1 if axis == dim else 1 for axis in range(len(dims))])
    return gain


def scatter_about(own_key, dims, spread, bound, pieces=(), held_as=jnp.bfloat16):
    loudness = levels(own_key, dims, pieces, -0.22, 0.18) if pieces else 1.0
    values = jax.random.normal(own_key, dims, jnp.float32) * spread * loudness
    return jnp.minimum(jnp.maximum(values, -bound), bound).astype(held_as)


def setup_inputs(seed: int = 0) -> dict:
    arg_keys = jax.random.split(jax.random.key(seed), 5)
    a_blocks = scatter_about(arg_keys[0], (A_ROWS, A_COLS, BLOCK, BLOCK), 1.0, 6.0, ((0, 16), (1, 8)))
    a_pattern = draw_a_pattern(jax.random.fold_in(arg_keys[4], 71), 0)
    b_blocks = scatter_about(arg_keys[2], (B_ROWS, B_COLS, BLOCK, BLOCK), BLOCK ** -0.5, 0.5, ((0, 16), (1, 8)))
    b_pattern = draw_b_pattern(jax.random.fold_in(arg_keys[4], 71), 0)
    return {"a_blocks": a_blocks, "a_pattern": a_pattern, "b_blocks": b_blocks, "b_pattern": b_pattern}


def masked(blocks, pattern):
    return blocks * pattern[:, :, None, None].astype(blocks.dtype)


def reference(a_blocks, a_pattern, b_blocks, b_pattern):
    a_hat = masked(a_blocks, a_pattern)
    b_hat = masked(b_blocks, b_pattern)
    a_tiles = a_hat.reshape(N_ROW, BR, N_ROW, KS, BLOCK, BLOCK).transpose(0, 2, 1, 3, 4, 5)
    b_tiles = b_hat.reshape(N_ROW, KS, N_ROW, BC, BLOCK, BLOCK).transpose(0, 2, 1, 3, 4, 5)

    def tile_row(index):
        own_a = lax.dynamic_index_in_dim(a_tiles, index, 0, keepdims=False)
        own_b = lax.dynamic_index_in_dim(b_tiles, index, 0, keepdims=False)
        next_index = ((index + 1) % N_ROW).astype(jnp.int32)
        next_b = lax.dynamic_index_in_dim(b_tiles, next_index, 0, keepdims=False)
        later_a = jnp.roll(own_a, -1, axis=0)
        first_product = jnp.einsum('lrkxy,lkcyz->lrcxz', own_a.astype(jnp.float32), own_b.astype(jnp.float32))
        second_product = jnp.einsum('lrkxy,lkcyz->lrcxz', later_a.astype(jnp.float32), next_b.astype(jnp.float32))
        return first_product + second_product

    result = lax.map(tile_row, jnp.arange(N_ROW, dtype=jnp.int32))
    return result.transpose(0, 2, 1, 3, 4, 5).reshape(A_ROWS, B_COLS, BLOCK, BLOCK)
```

```python
import functools

import jax
import jax.numpy as jnp
from jax import lax
from jax.experimental import pallas as pl
from jax.experimental.pallas import tpu as pltpu
from jax.sharding import PartitionSpec as P

BR, KS, BC = 8, 16, 8
CAP = 16
BLOCK = 128
UNROLL = 4
PAIRS, TOUCHED, LIST = 8, 160, 256
ANY = pl.BlockSpec(memory_space=pl.ANY)
HBM = pl.BlockSpec(memory_space=pltpu.HBM)
SMEM = pl.BlockSpec(memory_space=pltpu.SMEM)


def passed_along(value, axis, steps):
    count = lax.axis_size(axis)
    pairs = [(source, (source + steps) % count) for source in range(count)]
    return lax.ppermute(value, axis, pairs)


def present(pattern, first_col, rows, cols, places, starts=None):
    count = jnp.int32(0)
    for row in range(rows):
        if starts is not None:
            starts[row] = count
        for col in range(cols):
            places[count] = row * cols + col
            count = count + pattern[row, first_col + col]
    if starts is not None:
        starts[rows] = count
    return count


def gather(pattern, first_col, rows, cols, source, packed, places, sem):
    count = present(pattern, first_col, rows, cols, places)

    def start(slot, carry):
        place = places[slot]
        pltpu.make_async_copy(
            source.at[place // cols, first_col + place % cols], packed.at[slot], sem
        ).start()
        return carry

    lax.fori_loop(0, count, start, 0)
    return count


def drain(count, source, target, sem):
    def wait(_, carry):
        pltpu.make_async_copy(source, target, sem).wait()
        return carry

    lax.fori_loop(0, count, wait, 0)


def pack_kernel(rows, cols, pattern, blocks, _, packed_0, packed_1, places_0, places_1, sem):
    count = gather(pattern, 0, rows, cols, blocks, packed_0, places_0, sem)
    count += gather(pattern, cols, rows, cols, blocks, packed_1, places_1, sem)
    drain(count, blocks.at[0, 0], packed_0.at[0], sem)


def pack(blocks, pattern, rows, cols, after):
    slots = pltpu.VMEM((CAP, BLOCK, BLOCK), blocks.dtype)
    return pl.pallas_call(
        functools.partial(pack_kernel, rows, cols),
        out_shape=(slots, slots),
        in_specs=[SMEM, HBM, ANY],
        out_specs=(ANY, ANY),
        scratch_shapes=[
            pltpu.SMEM((CAP + 1,), jnp.int32),
            pltpu.SMEM((CAP + 1,), jnp.int32),
            pltpu.SemaphoreType.DMA,
        ],
        compiler_params=pltpu.CompilerParams(vmem_limit_bytes=56 * 2**20),
        name="pack",
    )(pattern, blocks, after)


def list_pairs(a_pattern, a_col, b_pattern, b_col, out, a_places, b_places, b_starts, seen):
    a_count = present(a_pattern, a_col, BR, KS, a_places)
    present(b_pattern, b_col, KS, BC, b_places, b_starts)
    for place in range(BR * BC):
        seen[place] = 0

    def over_a(a_slot, counts):
        place = a_places[a_slot]
        row, inner = place // KS, place % KS

        def over_b(b_slot, counts):
            pairs, touched = counts
            target = row * BC + b_places[b_slot] % BC
            out[PAIRS + pairs] = a_slot + b_slot * 256 + target * 65536
            out[TOUCHED + touched] = target
            touched = touched + 1 - seen[target]
            seen[target] = 1
            return pairs + 1, touched

        return lax.fori_loop(b_starts[inner], b_starts[inner + 1], over_b, counts)

    pairs, touched = lax.fori_loop(0, a_count, over_a, (jnp.int32(0), jnp.int32(0)))
    for extra in range(UNROLL - 1):
        out[PAIRS + pairs + extra] = BR * BC * 65536
    out[0] = (pairs + UNROLL - 1) // UNROLL
    out[1] = touched


def multiply(pairs, a_slots, b_slots, total, first_col):
    def step(index, carry):
        products = []
        for part in range(UNROLL):
            pair = pairs[PAIRS + index * UNROLL + part]
            a_slot, b_slot, target = pair % 256, (pair // 256) % 256, pair // 65536
            product = jnp.dot(a_slots[a_slot], b_slots[b_slot], preferred_element_type=jnp.float32)
            products.append((target // BC, first_col + target % BC, product))
        for row, col, product in products:
            total[row, col] += product
        return carry

    lax.fori_loop(0, pairs[0], step, 0)


LIST_SCRATCH = [
    pltpu.SMEM((CAP + 1,), jnp.int32),
    pltpu.SMEM((CAP + 1,), jnp.int32),
    pltpu.SMEM((KS + 1,), jnp.int32),
    pltpu.SMEM((BR * BC,), jnp.int32),
]


def later_lists_kernel(a_pattern, a_next, b_next, list_0, list_1, *scratch):
    list_pairs(a_pattern, KS, b_next, 0, list_0, *scratch)
    list_pairs(a_next, 0, b_next, BC, list_1, *scratch)


def later_lists(a_pattern, a_next, b_next):
    lists = jax.ShapeDtypeStruct((LIST,), jnp.int32)
    return pl.pallas_call(
        later_lists_kernel,
        out_shape=(lists, lists),
        in_specs=[SMEM] * 3,
        out_specs=(SMEM, SMEM),
        scratch_shapes=LIST_SCRATCH,
        name="later_lists",
    )(a_pattern, a_next, b_next)


def first_kernel(
    a_pattern, b_pattern, a_0, a_1, b_0, b_1, result,
    total, a_held, b_held, own_0, own_1, sems, *scratch,
):
    loads = [
        pltpu.make_async_copy(packed, held, sems.at[index])
        for index, (packed, held) in enumerate(
            [(a_0, a_held.at[0]), (b_0, b_held.at[0]), (a_1, a_held.at[1]), (b_1, b_held.at[1])]
        )
    ]
    for load in loads:
        load.start()

    def clear(row, carry):
        total[row] = jnp.zeros(total.shape[1:], total.dtype)
        return carry

    lax.fori_loop(0, BR, clear, 0)
    list_pairs(a_pattern, 0, b_pattern, 0, own_0, *scratch)
    list_pairs(a_pattern, KS, b_pattern, BC, own_1, *scratch)
    for load in loads:
        load.wait()
    multiply(own_0, a_held.at[0], b_held.at[0], total, 0)
    multiply(own_1, a_held.at[1], b_held.at[1], total, BC)
    store = pltpu.make_async_copy(total.at[pl.ds(0, BR)], result, sems.at[4])
    store.start()
    store.wait()


def first(a_pattern, b_pattern, a_0, a_1, b_0, b_1):
    return pl.pallas_call(
        first_kernel,
        out_shape=jax.ShapeDtypeStruct((BR, 2 * BC, BLOCK, BLOCK), jnp.float32),
        in_specs=[SMEM] * 2 + [ANY] * 4,
        out_specs=ANY,
        scratch_shapes=[
            pltpu.VMEM((BR + 1, 2 * BC, BLOCK, BLOCK), jnp.float32),
            pltpu.VMEM((2, CAP, BLOCK, BLOCK), jnp.bfloat16),
            pltpu.VMEM((2, CAP, BLOCK, BLOCK), jnp.bfloat16),
            pltpu.SMEM((LIST,), jnp.int32),
            pltpu.SMEM((LIST,), jnp.int32),
            pltpu.SemaphoreType.DMA((5,)),
            *LIST_SCRATCH,
        ],
        compiler_params=pltpu.CompilerParams(vmem_limit_bytes=24 * 2**20),
        cost_estimate=pl.CostEstimate(flops=0, bytes_accessed=20 * 2**20, transcendentals=0),
        name="first_product",
    )(a_pattern, b_pattern, a_0, a_1, b_0, b_1)


def add_kernel(first_col, pairs, a_slots, b_slots, _, result, total, a_held, b_held, sems):
    load_a = pltpu.make_async_copy(a_slots, a_held, sems.at[0])
    load_b = pltpu.make_async_copy(b_slots, b_held, sems.at[1])
    load_a.start()
    load_b.start()
    touched = pairs[1]

    def block(index):
        target = pairs[TOUCHED + index]
        row, col = target // BC, target % BC
        return result.at[row, first_col + col], total.at[row, col]

    def load(index, carry):
        there, here = block(index)
        pltpu.make_async_copy(there, here, sems.at[2]).start()
        return carry

    def store(index, carry):
        there, here = block(index)
        pltpu.make_async_copy(here, there, sems.at[3]).start()
        return carry

    lax.fori_loop(0, touched, load, 0)
    load_a.wait()
    load_b.wait()
    drain(touched, result.at[0, 0], total.at[0, 0], sems.at[2])
    multiply(pairs, a_held, b_held, total, 0)
    lax.fori_loop(0, touched, store, 0)
    drain(touched, total.at[0, 0], result.at[0, 0], sems.at[3])


def add(pairs, a_slots, b_slots, result, first_col):
    return pl.pallas_call(
        functools.partial(add_kernel, first_col),
        out_shape=jax.ShapeDtypeStruct(result.shape, result.dtype),
        in_specs=[SMEM, ANY, ANY, ANY],
        out_specs=ANY,
        scratch_shapes=[
            pltpu.VMEM((BR + 1, BC, BLOCK, BLOCK), jnp.float32),
            pltpu.VMEM((CAP, BLOCK, BLOCK), jnp.bfloat16),
            pltpu.VMEM((CAP, BLOCK, BLOCK), jnp.bfloat16),
            pltpu.SemaphoreType.DMA((4,)),
        ],
        input_output_aliases={3: 0},
        compiler_params=pltpu.CompilerParams(vmem_limit_bytes=16 * 2**20),
        name="second_product",
    )(pairs, a_slots, b_slots, result)


def shards(a_blocks, a_pattern, b_blocks, b_pattern):
    a_next = passed_along(a_pattern, "col", -1)
    b_next = passed_along(b_pattern, "row", -1)
    b_0, b_1 = pack(b_blocks, b_pattern, KS, BC, b_pattern)
    b_later_0 = passed_along(b_0, "row", -1)
    b_later_1 = passed_along(b_1, "row", -1)
    list_0, list_1 = later_lists(a_pattern, a_next, b_next)
    a_0, a_1 = pack(a_blocks, a_pattern, BR, KS, list_0)
    a_later = passed_along(a_0, "col", -1)
    result = first(a_pattern, b_pattern, a_0, a_1, b_0, b_1)
    result = add(list_0, a_1, b_later_0, result, 0)
    return add(list_1, a_later, b_later_1, result, BC)


def solution(mesh):
    return jax.shard_map(
        shards,
        mesh=mesh,
        in_specs=(
            P("row", "col", None, None),
            P("row", "col"),
            P("row", "col", None, None),
            P("row", "col"),
        ),
        out_specs=P("row", "col", None, None),
        check_vma=False,
    )
```

```python
import functools

import jax
import jax.numpy as jnp
from jax import lax
from jax.experimental import pallas as pl
from jax.experimental.pallas import tpu as pltpu
from jax.sharding import PartitionSpec as P

BR, KS, BC = 8, 16, 8
CAP = 16
BLOCK = 128
B_SENT = 8
A_PART = 8
MARKS = 16
UNROLL = 4
PAIRS, TOUCHED, PLACES, LIST = 8, 144, 208, 256
ANY = pl.BlockSpec(memory_space=pl.ANY)
SMEM = pl.BlockSpec(memory_space=pltpu.SMEM)
VMEM = pl.BlockSpec(memory_space=pltpu.VMEM)


def passed_along(value, axis, steps, senders=None):
    count = lax.axis_size(axis)
    pairs = [(source, (source + steps) % count) for source in range(count)]
    return lax.ppermute(value, axis, pairs if senders is None else pairs[senders::2])


def rows_of(slot, count=1):
    return pl.ds(pl.multiple_of(slot * BLOCK, BLOCK), count * BLOCK)


def scan(pattern, first_col, rows, cols, places, starts=None):
    count = jnp.int32(0)
    for row in range(rows):
        if starts is not None:
            starts[row] = count
        for col in range(cols):
            places[count] = row * cols + col
            count = count + pattern[row, first_col + col]
    if starts is not None:
        starts[rows] = count
    return count


def fetch(first, last, first_col, cols, source, places, target, first_slot, sem):
    def start(index, carry):
        place = places[index]
        block = source.at[place // cols, first_col + place % cols]
        pltpu.make_async_copy(block, target.at[rows_of(first_slot + index - first)], sem).start()
        return carry

    lax.fori_loop(first, last, start, 0)


def write_marks(pattern, marks, target, sem):
    rows, cols = pattern.shape
    marks[...] = jnp.zeros(marks.shape, marks.dtype)
    marks[:rows, :cols] = pattern[...].astype(jnp.float32).astype(marks.dtype)
    copy = pltpu.make_async_copy(marks, target.at[pl.ds(target.shape[0] - MARKS, MARKS)], sem)
    copy.start()
    return copy


def drain(count, source, target, sem):
    def wait(_, carry):
        pltpu.make_async_copy(source, target, sem).wait()
        return carry

    lax.fori_loop(0, count, wait, 0)


def pack_b_kernel(pattern, pattern_held, blocks, sent, extra, info, places_0, places_1, marks, sem, marks_sem):
    copy = write_marks(pattern_held, marks, sent, marks_sem)
    count_0 = scan(pattern, 0, KS, BC, places_0)
    fetch(0, count_0, 0, BC, blocks, places_0, sent, 0, sem)
    count_1 = scan(pattern, BC, KS, BC, places_1)
    fetch(0, jnp.minimum(count_1, B_SENT), BC, BC, blocks, places_1, sent, 2 * B_SENT, sem)
    rest_0 = jnp.maximum(count_0 - B_SENT, 0)
    rest = rest_0 + jnp.maximum(count_1 - B_SENT, 0)
    last = jnp.minimum(count_1, 2 * B_SENT - rest_0)
    fetch(B_SENT, last, BC, BC, blocks, places_1, sent, B_SENT + rest_0, sem)
    fetch(jnp.maximum(last, B_SENT), count_1, BC, BC, blocks, places_1, extra, 0, sem)
    info[0] = (rest > B_SENT).astype(jnp.int32)
    drain(count_0 + count_1, blocks.at[0, 0], sent.at[rows_of(0)], sem)
    copy.wait()


def slots(count, marks=0):
    return pltpu.VMEM((count * BLOCK + marks, BLOCK), jnp.bfloat16)


INFO = jax.ShapeDtypeStruct((8,), jnp.int32)
PACK_PARAMS = pltpu.CompilerParams(vmem_limit_bytes=56 * 2**20)


def pack_b(blocks, pattern):
    return pl.pallas_call(
        pack_b_kernel,
        out_shape=(slots(3 * B_SENT, MARKS), slots(B_SENT), INFO),
        in_specs=[SMEM, VMEM, ANY],
        out_specs=(ANY, ANY, SMEM),
        scratch_shapes=[
            pltpu.SMEM((CAP + 1,), jnp.int32),
            pltpu.SMEM((CAP + 1,), jnp.int32),
            pltpu.VMEM((MARKS, BLOCK), jnp.bfloat16),
            pltpu.SemaphoreType.DMA,
            pltpu.SemaphoreType.DMA,
        ],
        compiler_params=PACK_PARAMS,
        name="pack_b",
    )(pattern, pattern, blocks)


def pack_a_kernel(pattern, pattern_held, blocks, part_0, part_1, places, marks, sems):
    copy = write_marks(pattern_held, marks, part_0, sems.at[1])
    count = scan(pattern, 0, BR, KS, places)
    fetch(0, jnp.minimum(count, A_PART), 0, KS, blocks, places, part_0, 0, sems.at[0])
    fetch(A_PART, count, 0, KS, blocks, places, part_1, 0, sems.at[0])
    drain(count, blocks.at[0, 0], part_1.at[rows_of(0)], sems.at[0])
    copy.wait()


def pack_a(blocks, pattern):
    return pl.pallas_call(
        pack_a_kernel,
        out_shape=(slots(A_PART, MARKS), slots(CAP - A_PART)),
        in_specs=[SMEM, VMEM, ANY],
        out_specs=(ANY, ANY),
        scratch_shapes=[
            pltpu.SMEM((CAP + 1,), jnp.int32),
            pltpu.VMEM((MARKS, BLOCK), jnp.bfloat16),
            pltpu.SemaphoreType.DMA((2,)),
        ],
        compiler_params=PACK_PARAMS,
        name="pack_a",
    )(pattern, pattern, blocks)


def list_pairs(a_count, a_places, b_places, b_starts, b_slot_of, out, seen):
    for place in range(BR * BC):
        seen[place] = 0

    def over_a(a_slot, counts):
        place = a_places[a_slot]
        row, inner = place // KS, place % KS

        def over_b(b_index, counts):
            pairs, touched = counts
            target = row * BC + b_places[b_index] % BC
            out[PAIRS + pairs] = a_slot + b_slot_of(b_index) * 256 + target * 65536
            out[TOUCHED + touched] = target
            touched = touched + 1 - seen[target]
            seen[target] = 1
            return pairs + 1, touched

        return lax.fori_loop(b_starts[inner], b_starts[inner + 1], over_b, counts)

    pairs, touched = lax.fori_loop(0, a_count, over_a, (jnp.int32(0), jnp.int32(0)))
    for extra in range(UNROLL - 1):
        out[PAIRS + pairs + extra] = BR * BC * 65536
    out[0] = (pairs + UNROLL - 1) // UNROLL
    out[1] = touched
    out[3] = a_count


LIST_SCRATCH = [
    pltpu.SMEM((CAP + 1,), jnp.int32),
    pltpu.SMEM((CAP + 1,), jnp.int32),
    pltpu.SMEM((KS + 1,), jnp.int32),
    pltpu.SMEM((BR * BC,), jnp.int32),
]


def rest_sent(flags, extra):
    def sent(senders, flag):
        return lax.cond(
            flag != 0,
            lambda value: passed_along(value, "row", -1, senders),
            jnp.zeros_like,
            extra,
        )

    def some(extra):
        return sent(1, flags[1]) + sent(0, flags[2])

    return lax.cond(flags[0] != 0, some, lambda extra: extra, extra)


def multiply(pairs, a_slots, b_slots, total, first_col):
    def step(index, carry):
        products = []
        for part in range(UNROLL):
            pair = pairs[PAIRS + index * UNROLL + part]
            a_slot, b_slot, target = pair % 256, (pair // 256) % 256, pair // 65536
            product = jnp.dot(
                a_slots[rows_of(a_slot), :], b_slots[rows_of(b_slot), :], preferred_element_type=jnp.float32
            )
            products.append((target // BC, first_col + target % BC, product))
        for row, col, product in products:
            total[row, col] += product
        return carry

    lax.fori_loop(0, pairs[0], step, 0)


def first_kernel(
    a_pattern, b_pattern, a_blocks, b_blocks, result,
    zeros, total, a_held, b_held, own_0, own_1, sems, a_places, b_places, b_starts, seen,
):
    zeros[...] = jnp.zeros(zeros.shape, zeros.dtype)
    clears = [pltpu.make_async_copy(zeros, result.at[row], sems.at[2]) for row in range(BR)]
    for clear in clears:
        clear.start()
    lists = (own_0, own_1)
    counts = []
    for tile, out in enumerate(lists):
        a_count = scan(a_pattern, tile * KS, BR, KS, a_places)
        fetch(0, a_count, tile * KS, KS, a_blocks, a_places, a_held.at[tile], 0, sems.at[tile])
        b_count = scan(b_pattern, tile * BC, KS, BC, b_places, starts=b_starts)
        fetch(0, b_count, tile * BC, BC, b_blocks, b_places, b_held.at[tile], 0, sems.at[tile])
        counts.append(a_count + b_count)
        list_pairs(a_count, a_places, b_places, b_starts, lambda index: index, out, seen)

        def clear(index, carry):
            target = out[TOUCHED + index]
            total[target // BC, tile * BC + target % BC] = jnp.zeros((BLOCK, BLOCK), total.dtype)
            return carry

        lax.fori_loop(0, out[1], clear, 0)
    for tile, out in enumerate(lists):
        drain(counts[tile], a_blocks.at[0, 0], a_held.at[0, rows_of(0)], sems.at[tile])
        multiply(out, a_held.at[tile], b_held.at[tile], total, tile * BC)
    for clear in clears:
        clear.wait()
    for tile, out in enumerate(lists):

        def store(index, carry):
            target = out[TOUCHED + index]
            row, col = target // BC, tile * BC + target % BC
            pltpu.make_async_copy(total.at[row, col], result.at[row, col], sems.at[3]).start()
            return carry

        lax.fori_loop(0, out[1], store, 0)
    drain(own_0[1] + own_1[1], total.at[0, 0], result.at[0, 0], sems.at[3])


def first(a_pattern, b_pattern, a_blocks, b_blocks):
    return pl.pallas_call(
        first_kernel,
        out_shape=jax.ShapeDtypeStruct((BR, 2 * BC, BLOCK, BLOCK), jnp.float32),
        in_specs=[SMEM, SMEM, ANY, ANY],
        out_specs=ANY,
        scratch_shapes=[
            pltpu.VMEM((2 * BC, BLOCK, BLOCK), jnp.float32),
            pltpu.VMEM((BR + 1, 2 * BC, BLOCK, BLOCK), jnp.float32),
            pltpu.VMEM((2, CAP * BLOCK, BLOCK), jnp.bfloat16),
            pltpu.VMEM((2, CAP * BLOCK, BLOCK), jnp.bfloat16),
            pltpu.SMEM((LIST,), jnp.int32),
            pltpu.SMEM((LIST,), jnp.int32),
            pltpu.SemaphoreType.DMA((4,)),
            *LIST_SCRATCH,
        ],
        compiler_params=pltpu.CompilerParams(vmem_limit_bytes=52 * 2**20),
        cost_estimate=pl.CostEstimate(flops=0, bytes_accessed=20 * 2**20, transcendentals=0),
        name="first_product",
    )(a_pattern, b_pattern, a_blocks, b_blocks)


def touched_blocks(pairs, first_col, result, total):
    def block(index):
        target = pairs[TOUCHED + index]
        row, col = target // BC, target % BC
        return result.at[row, first_col + col], total.at[row, col]

    def load(sem):
        def start(index, carry):
            there, here = block(index)
            pltpu.make_async_copy(there, here, sem).start()
            return carry

        lax.fori_loop(0, pairs[1], start, 0)

    def store(sem):
        def start(index, carry):
            there, here = block(index)
            pltpu.make_async_copy(here, there, sem).start()
            return carry

        lax.fori_loop(0, pairs[1], start, 0)

    return load, store


def read_marks(sent, marks, turned, sems):
    load = pltpu.make_async_copy(sent.at[pl.ds(sent.shape[0] - MARKS, MARKS)], marks, sems.at[0])
    load.start()

    def finish(pattern):
        load.wait()
        turned[...] = marks[...].astype(jnp.float32).astype(jnp.int32)
        copy = pltpu.make_async_copy(turned, pattern, sems.at[1])
        copy.start()
        copy.wait()

    return finish


READ_SCRATCH = [
    pltpu.VMEM((MARKS, BLOCK), jnp.bfloat16),
    pltpu.VMEM((MARKS, BLOCK), jnp.int32),
    pltpu.SMEM((MARKS, BLOCK), jnp.int32),
    pltpu.SemaphoreType.DMA((2,)),
]
B_PLACES, B_REST = 24, 48


def middle_kernel(
    a_pattern, b_info, b_sent, a_blocks, _, result, b_list, flags,
    total, a_held, b_held, pairs, marks, turned, b_next, mark_sems, sems, a_places, b_places, b_starts, seen,
):
    finish = read_marks(b_sent, marks, turned, mark_sems)
    load_b = pltpu.make_async_copy(b_sent.at[rows_of(0, 2 * B_SENT)], b_held, sems.at[0])
    load_b.start()
    a_count = scan(a_pattern, KS, BR, KS, a_places)
    fetch(0, a_count, KS, KS, a_blocks, a_places, a_held, 0, sems.at[1])
    finish(b_next)
    count_0 = scan(b_next, 0, KS, BC, b_places, starts=b_starts)
    list_pairs(a_count, a_places, b_places, b_starts, lambda index: index, pairs, seen)
    load, store = touched_blocks(pairs, 0, result, total)
    load(sems.at[2])

    count_1 = scan(b_next, BC, KS, BC, b_places, starts=b_starts)
    for row in range(KS + 1):
        b_list[row] = b_starts[row]
    for index in range(CAP):
        b_list[B_PLACES + index] = b_places[index]
    rest_0 = jnp.maximum(count_0 - B_SENT, 0)
    rest = rest_0 + jnp.maximum(count_1 - B_SENT, 0)
    b_list[B_REST] = rest_0
    goes, comes = b_info[0], (rest > B_SENT).astype(jnp.int32)
    odd_row = lax.axis_index("row") % 2 == 1
    flags[0] = goes | comes
    flags[1] = jnp.where(odd_row, goes, comes)
    flags[2] = jnp.where(odd_row, comes, goes)
    b_list[B_REST + 1] = comes

    load_b.wait()
    drain(a_count, a_blocks.at[0, 0], a_held.at[rows_of(0)], sems.at[1])
    drain(pairs[1], result.at[0, 0], total.at[0, 0], sems.at[2])
    multiply(pairs, a_held, b_held, total, 0)
    store(sems.at[3])
    drain(pairs[1], total.at[0, 0], result.at[0, 0], sems.at[3])


def middle(a_pattern, b_info, b_sent, a_blocks, result):
    return pl.pallas_call(
        middle_kernel,
        out_shape=(
            jax.ShapeDtypeStruct(result.shape, result.dtype),
            jax.ShapeDtypeStruct((64,), jnp.int32),
            INFO,
        ),
        in_specs=[SMEM, SMEM, ANY, ANY, ANY],
        out_specs=(ANY, SMEM, SMEM),
        scratch_shapes=[
            pltpu.VMEM((BR + 1, BC, BLOCK, BLOCK), jnp.float32),
            pltpu.VMEM((CAP * BLOCK, BLOCK), jnp.bfloat16),
            pltpu.VMEM((2 * B_SENT * BLOCK, BLOCK), jnp.bfloat16),
            pltpu.SMEM((LIST,), jnp.int32),
            *READ_SCRATCH,
            pltpu.SemaphoreType.DMA((4,)),
            *LIST_SCRATCH,
        ],
        input_output_aliases={4: 0},
        compiler_params=pltpu.CompilerParams(vmem_limit_bytes=40 * 2**20),
        name="second_product_first_tile",
    )(a_pattern, b_info, b_sent, a_blocks, result)


def last_list_kernel(b_list, a_sent, pairs, marks, turned, a_next, mark_sems, a_places, seen):
    finish = read_marks(a_sent, marks, turned, mark_sems)
    finish(a_next)
    a_count = scan(a_next, 0, BR, KS, a_places)
    rest_0 = b_list[B_REST]

    def b_slot_of(index):
        past = rest_0 + index - B_SENT
        later = jnp.where(past < B_SENT, past + B_SENT, past + 2 * B_SENT)
        return jnp.where(index < B_SENT, index + 2 * B_SENT, later)

    list_pairs(a_count, a_places, b_list.at[pl.ds(B_PLACES, CAP)], b_list, b_slot_of, pairs, seen)
    pairs[2] = b_list[B_REST + 1]


def last_list(b_list, a_sent):
    return pl.pallas_call(
        last_list_kernel,
        out_shape=jax.ShapeDtypeStruct((LIST,), jnp.int32),
        in_specs=[SMEM, ANY],
        out_specs=SMEM,
        scratch_shapes=[
            *READ_SCRATCH,
            pltpu.SMEM((CAP + 1,), jnp.int32),
            pltpu.SMEM((BR * BC,), jnp.int32),
        ],
        compiler_params=pltpu.CompilerParams(vmem_limit_bytes=16 * 2**20),
        name="last_list",
    )(b_list, a_sent)


def last_kernel(pairs, a_0, a_1, b_0, b_1, _, result, total, a_held, b_held, sems):
    loads = [
        pltpu.make_async_copy(a_0.at[rows_of(0, A_PART)], a_held.at[rows_of(0, A_PART)], sems.at[2]),
        pltpu.make_async_copy(a_1, a_held.at[rows_of(A_PART, CAP - A_PART)], sems.at[3]),
        pltpu.make_async_copy(
            b_0.at[rows_of(B_SENT, 2 * B_SENT)], b_held.at[rows_of(B_SENT, 2 * B_SENT)], sems.at[4]
        ),
    ]
    for each in loads:
        each.start()
    load, store = touched_blocks(pairs, BC, result, total)
    load(sems.at[0])

    @pl.when(pairs[2] != 0)
    def _():
        extra = pltpu.make_async_copy(b_1, b_held.at[rows_of(3 * B_SENT, B_SENT)], sems.at[5])
        extra.start()
        extra.wait()

    for each in loads:
        each.wait()
    drain(pairs[1], result.at[0, 0], total.at[0, 0], sems.at[0])
    multiply(pairs, a_held, b_held, total, 0)
    store(sems.at[1])
    drain(pairs[1], total.at[0, 0], result.at[0, 0], sems.at[1])


def last(pairs, a_0, a_1, b_0, b_1, result):
    return pl.pallas_call(
        last_kernel,
        out_shape=jax.ShapeDtypeStruct(result.shape, result.dtype),
        in_specs=[SMEM] + [ANY] * 5,
        out_specs=ANY,
        scratch_shapes=[
            pltpu.VMEM((BR + 1, BC, BLOCK, BLOCK), jnp.float32),
            pltpu.VMEM((CAP * BLOCK, BLOCK), jnp.bfloat16),
            pltpu.VMEM((4 * B_SENT * BLOCK, BLOCK), jnp.bfloat16),
            pltpu.SemaphoreType.DMA((6,)),
        ],
        input_output_aliases={5: 0},
        compiler_params=pltpu.CompilerParams(vmem_limit_bytes=16 * 2**20),
        name="second_product_second_tile",
    )(pairs, a_0, a_1, b_0, b_1, result)


def shards(a_blocks, a_pattern, b_blocks, b_pattern):
    b_sent, b_extra, b_info = pack_b(b_blocks, b_pattern)
    b_sent = passed_along(b_sent, "row", -1)
    a_sent_0, a_sent_1 = pack_a(a_blocks, a_pattern)
    a_sent_0 = passed_along(a_sent_0, "col", -1)
    result = first(a_pattern, b_pattern, a_blocks, b_blocks)
    a_sent_1, b_sent, result = lax.optimization_barrier((a_sent_1, b_sent, result))
    a_sent_1 = passed_along(a_sent_1, "col", -1)
    result, b_list, flags = middle(a_pattern, b_info, b_sent, a_blocks, result)
    b_extra = rest_sent(flags, b_extra)
    pairs = last_list(b_list, a_sent_0)
    return last(pairs, a_sent_0, a_sent_1, b_sent, b_extra, result)


def solution(mesh):
    return jax.shard_map(
        shards,
        mesh=mesh,
        in_specs=(
            P("row", "col", None, None),
            P("row", "col"),
            P("row", "col", None, None),
            P("row", "col"),
        ),
        out_specs=P("row", "col", None, None),
        check_vma=False,
    )
```

```python
import functools

import jax
import jax.numpy as jnp
from jax import lax
from jax.experimental import pallas as pl
from jax.experimental.pallas import tpu as pltpu
from jax.sharding import PartitionSpec as P

BR, KS, BC = 8, 16, 8
CAP = 16
BLOCK = 128
B_SENT = 8
A_PART = 8
MARKS = 16
UNROLL = 4
PAIRS, TOUCHED, LIST = 8, 144, 256
PLACES = 8
ANY = pl.BlockSpec(memory_space=pl.ANY)
SMEM = pl.BlockSpec(memory_space=pltpu.SMEM)
VMEM = pl.BlockSpec(memory_space=pltpu.VMEM)


def passed_along(value, axis, steps, senders=None):
    count = lax.axis_size(axis)
    pairs = [(source, (source + steps) % count) for source in range(count)]
    return lax.ppermute(value, axis, pairs if senders is None else pairs[senders::2])


def rows_of(slot, count=1):
    return pl.ds(pl.multiple_of(slot * BLOCK, BLOCK), count * BLOCK)


def scan(pattern, first_col, rows, cols, places, starts=None):
    count = jnp.int32(0)
    for row in range(rows):
        if starts is not None:
            starts[row] = count
        for col in range(cols):
            places[count] = row * cols + col
            count = count + pattern[row, first_col + col]
    if starts is not None:
        starts[rows] = count
    return count


def fetch(first, last, first_col, cols, source, places, target, first_slot, sem):
    def start(index, carry):
        place = places[index]
        block = source.at[place // cols, first_col + place % cols]
        pltpu.make_async_copy(block, target.at[rows_of(first_slot + index - first)], sem).start()
        return carry

    lax.fori_loop(first, last, start, 0)


def write_marks(pattern, marks, target, sem):
    rows, cols = pattern.shape
    marks[...] = jnp.zeros(marks.shape, marks.dtype)
    marks[:rows, :cols] = pattern[...].astype(jnp.float32).astype(marks.dtype)
    copy = pltpu.make_async_copy(marks, target.at[pl.ds(target.shape[0] - MARKS, MARKS)], sem)
    copy.start()
    return copy


def drain(count, source, target, sem):
    def wait(_, carry):
        pltpu.make_async_copy(source, target, sem).wait()
        return carry

    lax.fori_loop(0, count, wait, 0)


def pack_b_kernel(pattern, pattern_held, blocks, sent, extra, info, places_0, places_1, marks, sem, marks_sem):
    copy = write_marks(pattern_held, marks, sent, marks_sem)
    count_0 = scan(pattern, 0, KS, BC, places_0)
    fetch(0, count_0, 0, BC, blocks, places_0, sent, 0, sem)
    count_1 = scan(pattern, BC, KS, BC, places_1)
    fetch(0, jnp.minimum(count_1, B_SENT), BC, BC, blocks, places_1, sent, 2 * B_SENT, sem)
    rest_0 = jnp.maximum(count_0 - B_SENT, 0)
    rest = rest_0 + jnp.maximum(count_1 - B_SENT, 0)
    last = jnp.minimum(count_1, 2 * B_SENT - rest_0)
    fetch(B_SENT, last, BC, BC, blocks, places_1, sent, B_SENT + rest_0, sem)
    fetch(jnp.maximum(last, B_SENT), count_1, BC, BC, blocks, places_1, extra, 0, sem)
    info[0] = (rest > B_SENT).astype(jnp.int32)
    drain(count_0 + count_1, blocks.at[0, 0], sent.at[rows_of(0)], sem)
    copy.wait()


def slots(count, marks=0):
    return pltpu.VMEM((count * BLOCK + marks, BLOCK), jnp.bfloat16)


INFO = jax.ShapeDtypeStruct((8,), jnp.int32)
PACK_PARAMS = pltpu.CompilerParams(vmem_limit_bytes=56 * 2**20)


def pack_b(blocks, pattern):
    return pl.pallas_call(
        pack_b_kernel,
        out_shape=(slots(3 * B_SENT, MARKS), slots(B_SENT), INFO),
        in_specs=[SMEM, VMEM, ANY],
        out_specs=(ANY, ANY, SMEM),
        scratch_shapes=[
            pltpu.SMEM((CAP + 1,), jnp.int32),
            pltpu.SMEM((CAP + 1,), jnp.int32),
            pltpu.VMEM((MARKS, BLOCK), jnp.bfloat16),
            pltpu.SemaphoreType.DMA,
            pltpu.SemaphoreType.DMA,
        ],
        compiler_params=PACK_PARAMS,
        name="pack_b",
    )(pattern, pattern, blocks)


def pack_a_kernel(pattern, pattern_held, blocks, part_0, part_1, places, marks, sems):
    copy = write_marks(pattern_held, marks, part_0, sems.at[1])
    count = scan(pattern, 0, BR, KS, places)
    fetch(0, jnp.minimum(count, A_PART), 0, KS, blocks, places, part_0, 0, sems.at[0])
    fetch(A_PART, count, 0, KS, blocks, places, part_1, 0, sems.at[0])
    drain(count, blocks.at[0, 0], part_1.at[rows_of(0)], sems.at[0])
    copy.wait()


def pack_a(blocks, pattern):
    return pl.pallas_call(
        pack_a_kernel,
        out_shape=(slots(A_PART, MARKS), slots(CAP - A_PART)),
        in_specs=[SMEM, VMEM, ANY],
        out_specs=(ANY, ANY),
        scratch_shapes=[
            pltpu.SMEM((CAP + 1,), jnp.int32),
            pltpu.VMEM((MARKS, BLOCK), jnp.bfloat16),
            pltpu.SemaphoreType.DMA((2,)),
        ],
        compiler_params=PACK_PARAMS,
        name="pack_a",
    )(pattern, pattern, blocks)


def list_pairs(a_count, a_places, b_places, b_starts, b_slot_of, out, seen):
    for place in range(BR * BC):
        seen[place] = 0

    def over_a(a_slot, counts):
        place = a_places[a_slot]
        row, inner = place // KS, place % KS

        def over_b(b_index, counts):
            pairs, touched = counts
            target = row * BC + b_places[b_index] % BC
            out[PAIRS + pairs] = a_slot + b_slot_of(b_index) * 256 + target * 65536
            out[TOUCHED + touched] = target
            touched = touched + 1 - seen[target]
            seen[target] = 1
            return pairs + 1, touched

        return lax.fori_loop(b_starts[inner], b_starts[inner + 1], over_b, counts)

    pairs, touched = lax.fori_loop(0, a_count, over_a, (jnp.int32(0), jnp.int32(0)))
    for extra in range(UNROLL - 1):
        out[PAIRS + pairs + extra] = BR * BC * 65536
    out[0] = (pairs + UNROLL - 1) // UNROLL
    out[1] = touched


LIST_SCRATCH = [
    pltpu.SMEM((CAP + 1,), jnp.int32),
    pltpu.SMEM((CAP + 1,), jnp.int32),
    pltpu.SMEM((KS + 1,), jnp.int32),
    pltpu.SMEM((BR * BC,), jnp.int32),
]


def rest_sent(flags, extra):
    def sent(senders, flag):
        return lax.cond(
            flag != 0,
            lambda value: passed_along(value, "row", -1, senders),
            jnp.zeros_like,
            extra,
        )

    def some(extra):
        return sent(1, flags[1]) + sent(0, flags[2])

    return lax.cond(flags[0] != 0, some, lambda extra: extra, extra)


def multiply(pairs, a_slots, b_slots, total, first_col):
    def step(index, carry):
        products = []
        for part in range(UNROLL):
            pair = pairs[PAIRS + index * UNROLL + part]
            a_slot, b_slot, target = pair % 256, (pair // 256) % 256, pair // 65536
            product = jnp.dot(
                a_slots[rows_of(a_slot), :], b_slots[rows_of(b_slot), :], preferred_element_type=jnp.float32
            )
            products.append((target // BC, first_col + target % BC, product))
        for row, col, product in products:
            total[row, col] += product
        return carry

    lax.fori_loop(0, pairs[0], step, 0)


def first_kernel(
    a_pattern, b_pattern, a_blocks, b_blocks, result, own, own_places,
    zeros, total, a_held, b_held, own_0, own_1, sems, a_places, b_places, b_starts, seen,
):
    zeros[...] = jnp.zeros(zeros.shape, zeros.dtype)
    clears = [pltpu.make_async_copy(zeros, result.at[row], sems.at[2]) for row in range(BR)]
    for clear in clears:
        clear.start()
    lists = (own_0, own_1)
    counts = []
    for tile, out in enumerate(lists):
        a_count = scan(a_pattern, tile * KS, BR, KS, a_places)
        fetch(0, a_count, tile * KS, KS, a_blocks, a_places, a_held.at[tile], 0, sems.at[tile])
        b_count = scan(b_pattern, tile * BC, KS, BC, b_places, starts=b_starts)
        fetch(0, b_count, tile * BC, BC, b_blocks, b_places, b_held.at[tile], 0, sems.at[tile])
        counts.append(a_count + b_count)
        own_places[0] = a_count
        for slot in range(CAP):
            own_places[PLACES + slot] = a_places[slot]
        list_pairs(a_count, a_places, b_places, b_starts, lambda index: index, out, seen)

        def clear(index, carry):
            target = out[TOUCHED + index]
            total[target // BC, tile * BC + target % BC] = jnp.zeros((BLOCK, BLOCK), total.dtype)
            return carry

        lax.fori_loop(0, out[1], clear, 0)
    for tile, out in enumerate(lists):
        drain(counts[tile], a_blocks.at[0, 0], a_held.at[0, rows_of(0)], sems.at[tile])
        if tile == 1:
            keep = pltpu.make_async_copy(a_held.at[1], own, sems.at[4])
            keep.start()
        multiply(out, a_held.at[tile], b_held.at[tile], total, tile * BC)
    for clear in clears:
        clear.wait()
    for tile, out in enumerate(lists):

        def store(index, carry):
            target = out[TOUCHED + index]
            row, col = target // BC, tile * BC + target % BC
            pltpu.make_async_copy(total.at[row, col], result.at[row, col], sems.at[3]).start()
            return carry

        lax.fori_loop(0, out[1], store, 0)
    drain(own_0[1] + own_1[1], total.at[0, 0], result.at[0, 0], sems.at[3])
    keep.wait()


def first(a_pattern, b_pattern, a_blocks, b_blocks):
    return pl.pallas_call(
        first_kernel,
        out_shape=(
            jax.ShapeDtypeStruct((BR, 2 * BC, BLOCK, BLOCK), jnp.float32),
            slots(CAP),
            jax.ShapeDtypeStruct((PLACES + CAP,), jnp.int32),
        ),
        in_specs=[SMEM, SMEM, ANY, ANY],
        out_specs=(ANY, ANY, SMEM),
        scratch_shapes=[
            pltpu.VMEM((2 * BC, BLOCK, BLOCK), jnp.float32),
            pltpu.VMEM((BR + 1, 2 * BC, BLOCK, BLOCK), jnp.float32),
            pltpu.VMEM((2, CAP * BLOCK, BLOCK), jnp.bfloat16),
            pltpu.VMEM((2, CAP * BLOCK, BLOCK), jnp.bfloat16),
            pltpu.SMEM((LIST,), jnp.int32),
            pltpu.SMEM((LIST,), jnp.int32),
            pltpu.SemaphoreType.DMA((5,)),
            *LIST_SCRATCH,
        ],
        compiler_params=pltpu.CompilerParams(vmem_limit_bytes=52 * 2**20),
        name="first_product",
    )(a_pattern, b_pattern, a_blocks, b_blocks)


def touched_blocks(pairs, first_col, result, total):
    def block(index):
        target = pairs[TOUCHED + index]
        row, col = target // BC, target % BC
        return result.at[row, first_col + col], total.at[row, col]

    def load(sem):
        def start(index, carry):
            there, here = block(index)
            pltpu.make_async_copy(there, here, sem).start()
            return carry

        lax.fori_loop(0, pairs[1], start, 0)

    def store(sem):
        def start(index, carry):
            there, here = block(index)
            pltpu.make_async_copy(here, there, sem).start()
            return carry

        lax.fori_loop(0, pairs[1], start, 0)

    return load, store


def read_marks(sent, marks, turned, sems):
    load = pltpu.make_async_copy(sent.at[pl.ds(sent.shape[0] - MARKS, MARKS)], marks, sems.at[0])
    load.start()

    def finish(pattern):
        load.wait()
        turned[...] = marks[...].astype(jnp.float32).astype(jnp.int32)
        copy = pltpu.make_async_copy(turned, pattern, sems.at[1])
        copy.start()
        copy.wait()

    return finish


READ_SCRATCH = [
    pltpu.VMEM((MARKS, BLOCK), jnp.bfloat16),
    pltpu.VMEM((MARKS, BLOCK), jnp.int32),
    pltpu.SMEM((MARKS, BLOCK), jnp.int32),
    pltpu.SemaphoreType.DMA((2,)),
]
B_PLACES, B_REST = 24, 48


def middle_kernel(
    own_places, b_info, own, b_sent, _, result, b_list, flags,
    total, a_held, b_held, pairs, marks, turned, b_next, mark_sems, sems, b_places, b_starts, seen,
):
    finish = read_marks(b_sent, marks, turned, mark_sems)
    load_b = pltpu.make_async_copy(b_sent.at[rows_of(0, 2 * B_SENT)], b_held, sems.at[0])
    load_b.start()
    load_a = pltpu.make_async_copy(own, a_held, sems.at[1])
    load_a.start()
    finish(b_next)
    count_0 = scan(b_next, 0, KS, BC, b_places, starts=b_starts)
    a_places = own_places.at[pl.ds(PLACES, CAP)]
    list_pairs(own_places[0], a_places, b_places, b_starts, lambda index: index, pairs, seen)
    load, store = touched_blocks(pairs, 0, result, total)
    load(sems.at[2])

    count_1 = scan(b_next, BC, KS, BC, b_places, starts=b_starts)
    for row in range(KS + 1):
        b_list[row] = b_starts[row]
    for index in range(CAP):
        b_list[B_PLACES + index] = b_places[index]
    rest_0 = jnp.maximum(count_0 - B_SENT, 0)
    rest = rest_0 + jnp.maximum(count_1 - B_SENT, 0)
    b_list[B_REST] = rest_0
    goes, comes = b_info[0], (rest > B_SENT).astype(jnp.int32)
    odd_row = lax.axis_index("row") % 2 == 1
    flags[0] = goes | comes
    flags[1] = jnp.where(odd_row, goes, comes)
    flags[2] = jnp.where(odd_row, comes, goes)
    b_list[B_REST + 1] = comes

    load_b.wait()
    load_a.wait()
    drain(pairs[1], result.at[0, 0], total.at[0, 0], sems.at[2])
    multiply(pairs, a_held, b_held, total, 0)
    store(sems.at[3])
    drain(pairs[1], total.at[0, 0], result.at[0, 0], sems.at[3])


def middle(own_places, b_info, own, b_sent, result):
    return pl.pallas_call(
        middle_kernel,
        out_shape=(
            jax.ShapeDtypeStruct(result.shape, result.dtype),
            jax.ShapeDtypeStruct((64,), jnp.int32),
            INFO,
        ),
        in_specs=[SMEM, SMEM, ANY, ANY, ANY],
        out_specs=(ANY, SMEM, SMEM),
        scratch_shapes=[
            pltpu.VMEM((BR + 1, BC, BLOCK, BLOCK), jnp.float32),
            pltpu.VMEM((CAP * BLOCK, BLOCK), jnp.bfloat16),
            pltpu.VMEM((2 * B_SENT * BLOCK, BLOCK), jnp.bfloat16),
            pltpu.SMEM((LIST,), jnp.int32),
            *READ_SCRATCH,
            pltpu.SemaphoreType.DMA((4,)),
            *LIST_SCRATCH[1:],
        ],
        input_output_aliases={4: 0},
        compiler_params=pltpu.CompilerParams(vmem_limit_bytes=16 * 2**20),
        name="second_product_first_tile",
    )(own_places, b_info, own, b_sent, result)


def last_list_kernel(b_list, a_sent, pairs, marks, turned, a_next, mark_sems, a_places, seen):
    finish = read_marks(a_sent, marks, turned, mark_sems)
    finish(a_next)
    a_count = scan(a_next, 0, BR, KS, a_places)
    rest_0 = b_list[B_REST]

    def b_slot_of(index):
        past = rest_0 + index - B_SENT
        later = jnp.where(past < B_SENT, past + B_SENT, past + 2 * B_SENT)
        return jnp.where(index < B_SENT, index + 2 * B_SENT, later)

    list_pairs(a_count, a_places, b_list.at[pl.ds(B_PLACES, CAP)], b_list, b_slot_of, pairs, seen)
    pairs[2] = b_list[B_REST + 1]


def last_list(b_list, a_sent):
    return pl.pallas_call(
        last_list_kernel,
        out_shape=jax.ShapeDtypeStruct((LIST,), jnp.int32),
        in_specs=[SMEM, ANY],
        out_specs=SMEM,
        scratch_shapes=[
            *READ_SCRATCH,
            pltpu.SMEM((CAP + 1,), jnp.int32),
            pltpu.SMEM((BR * BC,), jnp.int32),
        ],
        compiler_params=pltpu.CompilerParams(vmem_limit_bytes=16 * 2**20),
        name="last_list",
    )(b_list, a_sent)


def last_kernel(pairs, a_0, a_1, b_0, b_1, _, result, total, a_held, b_held, sems):
    loads = [
        pltpu.make_async_copy(a_0.at[rows_of(0, A_PART)], a_held.at[rows_of(0, A_PART)], sems.at[2]),
        pltpu.make_async_copy(a_1, a_held.at[rows_of(A_PART, CAP - A_PART)], sems.at[3]),
        pltpu.make_async_copy(
            b_0.at[rows_of(B_SENT, 2 * B_SENT)], b_held.at[rows_of(B_SENT, 2 * B_SENT)], sems.at[4]
        ),
    ]
    for each in loads:
        each.start()
    load, store = touched_blocks(pairs, BC, result, total)
    load(sems.at[0])

    @pl.when(pairs[2] != 0)
    def _():
        extra = pltpu.make_async_copy(b_1, b_held.at[rows_of(3 * B_SENT, B_SENT)], sems.at[5])
        extra.start()
        extra.wait()

    for each in loads:
        each.wait()
    drain(pairs[1], result.at[0, 0], total.at[0, 0], sems.at[0])
    multiply(pairs, a_held, b_held, total, 0)
    store(sems.at[1])
    drain(pairs[1], total.at[0, 0], result.at[0, 0], sems.at[1])


def last(pairs, a_0, a_1, b_0, b_1, result):
    return pl.pallas_call(
        last_kernel,
        out_shape=jax.ShapeDtypeStruct(result.shape, result.dtype),
        in_specs=[SMEM] + [ANY] * 5,
        out_specs=ANY,
        scratch_shapes=[
            pltpu.VMEM((BR + 1, BC, BLOCK, BLOCK), jnp.float32),
            pltpu.VMEM((CAP * BLOCK, BLOCK), jnp.bfloat16),
            pltpu.VMEM((4 * B_SENT * BLOCK, BLOCK), jnp.bfloat16),
            pltpu.SemaphoreType.DMA((6,)),
        ],
        input_output_aliases={5: 0},
        compiler_params=pltpu.CompilerParams(vmem_limit_bytes=16 * 2**20),
        name="second_product_second_tile",
    )(pairs, a_0, a_1, b_0, b_1, result)


def shards(a_blocks, a_pattern, b_blocks, b_pattern):
    b_sent, b_extra, b_info = pack_b(b_blocks, b_pattern)
    b_sent = passed_along(b_sent, "row", -1)
    a_sent_0, a_sent_1 = pack_a(a_blocks, a_pattern)
    a_sent_0 = passed_along(a_sent_0, "col", -1)
    result, own, own_places = first(a_pattern, b_pattern, a_blocks, b_blocks)
    a_sent_1, result = lax.optimization_barrier((a_sent_1, result))
    a_sent_1 = passed_along(a_sent_1, "col", -1)
    result, b_list, flags = middle(own_places, b_info, own, b_sent, result)
    b_extra = rest_sent(flags, b_extra)
    pairs = last_list(b_list, a_sent_0)
    return last(pairs, a_sent_0, a_sent_1, b_sent, b_extra, result)


def solution(mesh):
    return jax.shard_map(
        shards,
        mesh=mesh,
        in_specs=(
            P("row", "col", None, None),
            P("row", "col"),
            P("row", "col", None, None),
            P("row", "col"),
        ),
        out_specs=P("row", "col", None, None),
        check_vma=False,
    )
```

```python
import functools

import jax
import jax.numpy as jnp
from jax import lax
from jax.experimental import pallas as pl
from jax.experimental.pallas import tpu as pltpu
from jax.sharding import PartitionSpec as P

BR, KS, BC = 8, 16, 8
CAP = 16
BLOCK = 128
B_SENT = 8
A_PART = 8
MARKS = 16
UNROLL = 2
PAIRS, TOUCHED, LIST = 8, 144, 256
PLACES = 8
ANY = pl.BlockSpec(memory_space=pl.ANY)
SMEM = pl.BlockSpec(memory_space=pltpu.SMEM)
VMEM = pl.BlockSpec(memory_space=pltpu.VMEM)


def passed_along(value, axis, steps, senders=None):
    count = lax.axis_size(axis)
    pairs = [(source, (source + steps) % count) for source in range(count)]
    return lax.ppermute(value, axis, pairs if senders is None else pairs[senders::2])


def rows_of(slot, count=1):
    return pl.ds(pl.multiple_of(slot * BLOCK, BLOCK), count * BLOCK)


def scan(pattern, first_col, rows, cols, places, starts=None):
    count = jnp.int32(0)
    for row in range(rows):
        if starts is not None:
            starts[row] = count
        for col in range(cols):
            places[count] = row * cols + col
            count = count + pattern[row, first_col + col]
    if starts is not None:
        starts[rows] = count
    return count


def fetch(first, last, first_col, cols, source, places, target, first_slot, sem):
    def start(index, carry):
        place = places[index]
        block = source.at[place // cols, first_col + place % cols]
        pltpu.make_async_copy(block, target.at[rows_of(first_slot + index - first)], sem).start()
        return carry

    lax.fori_loop(first, last, start, 0)


def write_marks(pattern, marks, target, sem):
    rows, cols = pattern.shape
    marks[...] = jnp.zeros(marks.shape, marks.dtype)
    marks[:rows, :cols] = pattern[...].astype(jnp.float32).astype(marks.dtype)
    copy = pltpu.make_async_copy(marks, target.at[pl.ds(target.shape[0] - MARKS, MARKS)], sem)
    copy.start()
    return copy


def drain(count, source, target, sem):
    def wait(_, carry):
        pltpu.make_async_copy(source, target, sem).wait()
        return carry

    lax.fori_loop(0, count, wait, 0)


def pack_b_kernel(pattern, pattern_held, blocks, sent, extra, info, places_0, places_1, marks, sem, marks_sem):
    copy = write_marks(pattern_held, marks, sent, marks_sem)
    count_0 = scan(pattern, 0, KS, BC, places_0)
    fetch(0, count_0, 0, BC, blocks, places_0, sent, 0, sem)
    count_1 = scan(pattern, BC, KS, BC, places_1)
    fetch(0, jnp.minimum(count_1, B_SENT), BC, BC, blocks, places_1, sent, 2 * B_SENT, sem)
    rest_0 = jnp.maximum(count_0 - B_SENT, 0)
    rest = rest_0 + jnp.maximum(count_1 - B_SENT, 0)
    last = jnp.minimum(count_1, 2 * B_SENT - rest_0)
    fetch(B_SENT, last, BC, BC, blocks, places_1, sent, B_SENT + rest_0, sem)
    fetch(jnp.maximum(last, B_SENT), count_1, BC, BC, blocks, places_1, extra, 0, sem)
    info[0] = (rest > B_SENT).astype(jnp.int32)
    drain(count_0 + count_1, blocks.at[0, 0], sent.at[rows_of(0)], sem)
    copy.wait()


def slots(count, marks=0):
    return pltpu.VMEM((count * BLOCK + marks, BLOCK), jnp.bfloat16)


INFO = jax.ShapeDtypeStruct((8,), jnp.int32)
PACK_PARAMS = pltpu.CompilerParams(vmem_limit_bytes=56 * 2**20)


def pack_b(blocks, pattern):
    return pl.pallas_call(
        pack_b_kernel,
        out_shape=(slots(3 * B_SENT, MARKS), slots(B_SENT), INFO),
        in_specs=[SMEM, VMEM, ANY],
        out_specs=(ANY, ANY, SMEM),
        scratch_shapes=[
            pltpu.SMEM((CAP + 1,), jnp.int32),
            pltpu.SMEM((CAP + 1,), jnp.int32),
            pltpu.VMEM((MARKS, BLOCK), jnp.bfloat16),
            pltpu.SemaphoreType.DMA,
            pltpu.SemaphoreType.DMA,
        ],
        compiler_params=PACK_PARAMS,
        name="pack_b",
    )(pattern, pattern, blocks)


def pack_a_kernel(pattern, pattern_held, blocks, part_0, part_1, places, marks, sems):
    copy = write_marks(pattern_held, marks, part_0, sems.at[1])
    count = scan(pattern, 0, BR, KS, places)
    fetch(0, jnp.minimum(count, A_PART), 0, KS, blocks, places, part_0, 0, sems.at[0])
    fetch(A_PART, count, 0, KS, blocks, places, part_1, 0, sems.at[0])
    drain(count, blocks.at[0, 0], part_1.at[rows_of(0)], sems.at[0])
    copy.wait()


def pack_a(blocks, pattern):
    return pl.pallas_call(
        pack_a_kernel,
        out_shape=(slots(A_PART, MARKS), slots(CAP - A_PART)),
        in_specs=[SMEM, VMEM, ANY],
        out_specs=(ANY, ANY),
        scratch_shapes=[
            pltpu.SMEM((CAP + 1,), jnp.int32),
            pltpu.VMEM((MARKS, BLOCK), jnp.bfloat16),
            pltpu.SemaphoreType.DMA((2,)),
        ],
        compiler_params=PACK_PARAMS,
        name="pack_a",
    )(pattern, pattern, blocks)


def list_pairs(a_count, a_places, b_places, b_starts, b_slot_of, out, seen):
    for place in range(BR * BC):
        seen[place] = 0

    def over_a(a_slot, counts):
        place = a_places[a_slot]
        row, inner = place // KS, place % KS

        def over_b(b_index, counts):
            pairs, touched = counts
            target = row * BC + b_places[b_index] % BC
            out[PAIRS + pairs] = a_slot + b_slot_of(b_index) * 256 + target * 65536
            out[TOUCHED + touched] = target
            touched = touched + 1 - seen[target]
            seen[target] = 1
            return pairs + 1, touched

        return lax.fori_loop(b_starts[inner], b_starts[inner + 1], over_b, counts)

    pairs, touched = lax.fori_loop(0, a_count, over_a, (jnp.int32(0), jnp.int32(0)))
    for extra in range(UNROLL - 1):
        out[PAIRS + pairs + extra] = BR * BC * 65536
    out[0] = (pairs + UNROLL - 1) // UNROLL
    out[1] = touched


LIST_SCRATCH = [
    pltpu.SMEM((CAP + 1,), jnp.int32),
    pltpu.SMEM((CAP + 1,), jnp.int32),
    pltpu.SMEM((KS + 1,), jnp.int32),
    pltpu.SMEM((BR * BC,), jnp.int32),
]


def rest_sent(flags, extra):
    def sent(senders, flag):
        return lax.cond(
            flag != 0,
            lambda value: passed_along(value, "row", -1, senders),
            jnp.zeros_like,
            extra,
        )

    def some(extra):
        return sent(1, flags[1]) + sent(0, flags[2])

    return lax.cond(flags[0] != 0, some, lambda extra: extra, extra)


def multiply(pairs, a_slots, b_slots, total, first_col):
    def step(index, carry):
        products = []
        for part in range(UNROLL):
            pair = pairs[PAIRS + index * UNROLL + part]
            a_slot, b_slot, target = pair % 256, (pair // 256) % 256, pair // 65536
            product = jnp.dot(
                a_slots[rows_of(a_slot), :], b_slots[rows_of(b_slot), :], preferred_element_type=jnp.float32
            )
            products.append((target // BC, first_col + target % BC, product))
        for row, col, product in products:
            total[row, col] += product
        return carry

    lax.fori_loop(0, pairs[0], step, 0)


def first_kernel(
    a_pattern, b_pattern, a_blocks, b_blocks, result, own, own_places,
    zeros, total, a_held, b_held, own_0, own_1, sems, a_places, b_places, b_starts, seen,
):
    zeros[...] = jnp.zeros(zeros.shape, zeros.dtype)
    clears = [pltpu.make_async_copy(zeros, result.at[row], sems.at[2]) for row in range(BR)]
    for clear in clears:
        clear.start()
    lists = (own_0, own_1)
    counts = []
    for tile, out in enumerate(lists):
        a_count = scan(a_pattern, tile * KS, BR, KS, a_places)
        fetch(0, a_count, tile * KS, KS, a_blocks, a_places, a_held.at[tile], 0, sems.at[tile])
        b_count = scan(b_pattern, tile * BC, KS, BC, b_places, starts=b_starts)
        fetch(0, b_count, tile * BC, BC, b_blocks, b_places, b_held.at[tile], 0, sems.at[tile])
        counts.append(a_count + b_count)
        own_places[0] = a_count
        for slot in range(CAP):
            own_places[PLACES + slot] = a_places[slot]
        list_pairs(a_count, a_places, b_places, b_starts, lambda index: index, out, seen)

        def clear(index, carry):
            target = out[TOUCHED + index]
            total[target // BC, tile * BC + target % BC] = jnp.zeros((BLOCK, BLOCK), total.dtype)
            return carry

        lax.fori_loop(0, out[1], clear, 0)
    for tile, out in enumerate(lists):
        drain(counts[tile], a_blocks.at[0, 0], a_held.at[0, rows_of(0)], sems.at[tile])
        if tile == 1:
            keep = pltpu.make_async_copy(a_held.at[1], own, sems.at[4])
            keep.start()
        multiply(out, a_held.at[tile], b_held.at[tile], total, tile * BC)
    for clear in clears:
        clear.wait()
    for tile, out in enumerate(lists):

        def store(index, carry):
            target = out[TOUCHED + index]
            row, col = target // BC, tile * BC + target % BC
            pltpu.make_async_copy(total.at[row, col], result.at[row, col], sems.at[3]).start()
            return carry

        lax.fori_loop(0, out[1], store, 0)
    drain(own_0[1] + own_1[1], total.at[0, 0], result.at[0, 0], sems.at[3])
    keep.wait()


def first(a_pattern, b_pattern, a_blocks, b_blocks):
    return pl.pallas_call(
        first_kernel,
        out_shape=(
            jax.ShapeDtypeStruct((BR, 2 * BC, BLOCK, BLOCK), jnp.float32),
            slots(CAP),
            jax.ShapeDtypeStruct((PLACES + CAP,), jnp.int32),
        ),
        in_specs=[SMEM, SMEM, ANY, ANY],
        out_specs=(ANY, ANY, SMEM),
        scratch_shapes=[
            pltpu.VMEM((2 * BC, BLOCK, BLOCK), jnp.float32),
            pltpu.VMEM((BR + 1, 2 * BC, BLOCK, BLOCK), jnp.float32),
            pltpu.VMEM((2, CAP * BLOCK, BLOCK), jnp.bfloat16),
            pltpu.VMEM((2, CAP * BLOCK, BLOCK), jnp.bfloat16),
            pltpu.SMEM((LIST,), jnp.int32),
            pltpu.SMEM((LIST,), jnp.int32),
            pltpu.SemaphoreType.DMA((5,)),
            *LIST_SCRATCH,
        ],
        compiler_params=pltpu.CompilerParams(vmem_limit_bytes=52 * 2**20),
        name="first_product",
    )(a_pattern, b_pattern, a_blocks, b_blocks)


def touched_blocks(pairs, first_col, result, total):
    def block(index):
        target = pairs[TOUCHED + index]
        row, col = target // BC, target % BC
        return result.at[row, first_col + col], total.at[row, col]

    def load(sem):
        def start(index, carry):
            there, here = block(index)
            pltpu.make_async_copy(there, here, sem).start()
            return carry

        lax.fori_loop(0, pairs[1], start, 0)

    def store(sem):
        def start(index, carry):
            there, here = block(index)
            pltpu.make_async_copy(here, there, sem).start()
            return carry

        lax.fori_loop(0, pairs[1], start, 0)

    return load, store


def read_marks(sent, marks, turned, sems):
    load = pltpu.make_async_copy(sent.at[pl.ds(sent.shape[0] - MARKS, MARKS)], marks, sems.at[0])
    load.start()

    def finish(pattern):
        load.wait()
        turned[...] = marks[...].astype(jnp.float32).astype(jnp.int32)
        copy = pltpu.make_async_copy(turned, pattern, sems.at[1])
        copy.start()
        copy.wait()

    return finish


READ_SCRATCH = [
    pltpu.VMEM((MARKS, BLOCK), jnp.bfloat16),
    pltpu.VMEM((MARKS, BLOCK), jnp.int32),
    pltpu.SMEM((MARKS, BLOCK), jnp.int32),
    pltpu.SemaphoreType.DMA((2,)),
]
B_PLACES, B_REST = 24, 48


def middle_kernel(
    own_places, b_info, own, b_sent, _, result, b_list, flags,
    total, a_held, b_held, pairs, marks, turned, b_next, mark_sems, sems, b_places, b_starts, seen,
):
    finish = read_marks(b_sent, marks, turned, mark_sems)
    load_b = pltpu.make_async_copy(b_sent.at[rows_of(0, 2 * B_SENT)], b_held, sems.at[0])
    load_b.start()
    load_a = pltpu.make_async_copy(own, a_held, sems.at[1])
    load_a.start()
    finish(b_next)
    count_0 = scan(b_next, 0, KS, BC, b_places, starts=b_starts)
    a_places = own_places.at[pl.ds(PLACES, CAP)]
    list_pairs(own_places[0], a_places, b_places, b_starts, lambda index: index, pairs, seen)
    load, store = touched_blocks(pairs, 0, result, total)
    load(sems.at[2])

    count_1 = scan(b_next, BC, KS, BC, b_places, starts=b_starts)
    for row in range(KS + 1):
        b_list[row] = b_starts[row]
    for index in range(CAP):
        b_list[B_PLACES + index] = b_places[index]
    rest_0 = jnp.maximum(count_0 - B_SENT, 0)
    rest = rest_0 + jnp.maximum(count_1 - B_SENT, 0)
    b_list[B_REST] = rest_0
    goes, comes = b_info[0], (rest > B_SENT).astype(jnp.int32)
    odd_row = lax.axis_index("row") % 2 == 1
    flags[0] = goes | comes
    flags[1] = jnp.where(odd_row, goes, comes)
    flags[2] = jnp.where(odd_row, comes, goes)
    b_list[B_REST + 1] = comes

    load_b.wait()
    load_a.wait()
    drain(pairs[1], result.at[0, 0], total.at[0, 0], sems.at[2])
    multiply(pairs, a_held, b_held, total, 0)
    store(sems.at[3])
    drain(pairs[1], total.at[0, 0], result.at[0, 0], sems.at[3])


def middle(own_places, b_info, own, b_sent, result):
    return pl.pallas_call(
        middle_kernel,
        out_shape=(
            jax.ShapeDtypeStruct(result.shape, result.dtype),
            jax.ShapeDtypeStruct((64,), jnp.int32),
            INFO,
        ),
        in_specs=[SMEM, SMEM, ANY, ANY, ANY],
        out_specs=(ANY, SMEM, SMEM),
        scratch_shapes=[
            pltpu.VMEM((BR + 1, BC, BLOCK, BLOCK), jnp.float32),
            pltpu.VMEM((CAP * BLOCK, BLOCK), jnp.bfloat16),
            pltpu.VMEM((2 * B_SENT * BLOCK, BLOCK), jnp.bfloat16),
            pltpu.SMEM((LIST,), jnp.int32),
            *READ_SCRATCH,
            pltpu.SemaphoreType.DMA((4,)),
            *LIST_SCRATCH[1:],
        ],
        input_output_aliases={4: 0},
        compiler_params=pltpu.CompilerParams(vmem_limit_bytes=16 * 2**20),
        name="second_product_first_tile",
    )(own_places, b_info, own, b_sent, result)


def last_list_kernel(b_list, a_sent, pairs, marks, turned, a_next, mark_sems, a_places, seen):
    finish = read_marks(a_sent, marks, turned, mark_sems)
    finish(a_next)
    a_count = scan(a_next, 0, BR, KS, a_places)
    rest_0 = b_list[B_REST]

    def b_slot_of(index):
        past = rest_0 + index - B_SENT
        later = jnp.where(past < B_SENT, past + B_SENT, past + 2 * B_SENT)
        return jnp.where(index < B_SENT, index + 2 * B_SENT, later)

    list_pairs(a_count, a_places, b_list.at[pl.ds(B_PLACES, CAP)], b_list, b_slot_of, pairs, seen)
    pairs[2] = b_list[B_REST + 1]


def last_list(b_list, a_sent):
    return pl.pallas_call(
        last_list_kernel,
        out_shape=jax.ShapeDtypeStruct((LIST,), jnp.int32),
        in_specs=[SMEM, ANY],
        out_specs=SMEM,
        scratch_shapes=[
            *READ_SCRATCH,
            pltpu.SMEM((CAP + 1,), jnp.int32),
            pltpu.SMEM((BR * BC,), jnp.int32),
        ],
        compiler_params=pltpu.CompilerParams(vmem_limit_bytes=16 * 2**20),
        name="last_list",
    )(b_list, a_sent)


def last_kernel(pairs, a_0, a_1, b_0, b_1, _, result, total, a_held, b_held, sems):
    loads = [
        pltpu.make_async_copy(a_0.at[rows_of(0, A_PART)], a_held.at[rows_of(0, A_PART)], sems.at[2]),
        pltpu.make_async_copy(a_1, a_held.at[rows_of(A_PART, CAP - A_PART)], sems.at[3]),
        pltpu.make_async_copy(
            b_0.at[rows_of(B_SENT, 2 * B_SENT)], b_held.at[rows_of(B_SENT, 2 * B_SENT)], sems.at[4]
        ),
    ]
    for each in loads:
        each.start()
    load, store = touched_blocks(pairs, BC, result, total)
    load(sems.at[0])

    @pl.when(pairs[2] != 0)
    def _():
        extra = pltpu.make_async_copy(b_1, b_held.at[rows_of(3 * B_SENT, B_SENT)], sems.at[5])
        extra.start()
        extra.wait()

    for each in loads:
        each.wait()
    drain(pairs[1], result.at[0, 0], total.at[0, 0], sems.at[0])
    multiply(pairs, a_held, b_held, total, 0)
    store(sems.at[1])
    drain(pairs[1], total.at[0, 0], result.at[0, 0], sems.at[1])


def last(pairs, a_0, a_1, b_0, b_1, result):
    return pl.pallas_call(
        last_kernel,
        out_shape=jax.ShapeDtypeStruct(result.shape, result.dtype),
        in_specs=[SMEM] + [ANY] * 5,
        out_specs=ANY,
        scratch_shapes=[
            pltpu.VMEM((BR + 1, BC, BLOCK, BLOCK), jnp.float32),
            pltpu.VMEM((CAP * BLOCK, BLOCK), jnp.bfloat16),
            pltpu.VMEM((4 * B_SENT * BLOCK, BLOCK), jnp.bfloat16),
            pltpu.SemaphoreType.DMA((6,)),
        ],
        input_output_aliases={5: 0},
        compiler_params=pltpu.CompilerParams(vmem_limit_bytes=16 * 2**20),
        name="second_product_second_tile",
    )(pairs, a_0, a_1, b_0, b_1, result)


def shards(a_blocks, a_pattern, b_blocks, b_pattern):
    b_sent, b_extra, b_info = pack_b(b_blocks, b_pattern)
    b_sent = passed_along(b_sent, "row", -1)
    a_sent_0, a_sent_1 = pack_a(a_blocks, a_pattern)
    a_sent_0 = passed_along(a_sent_0, "col", -1)
    result, own, own_places = first(a_pattern, b_pattern, a_blocks, b_blocks)
    a_sent_1, result = lax.optimization_barrier((a_sent_1, result))
    a_sent_1 = passed_along(a_sent_1, "col", -1)
    result, b_list, flags = middle(own_places, b_info, own, b_sent, result)
    b_extra = rest_sent(flags, b_extra)
    pairs = last_list(b_list, a_sent_0)
    return last(pairs, a_sent_0, a_sent_1, b_sent, b_extra, result)


def solution(mesh):
    return jax.shard_map(
        shards,
        mesh=mesh,
        in_specs=(
            P("row", "col", None, None),
            P("row", "col"),
            P("row", "col", None, None),
            P("row", "col"),
        ),
        out_specs=P("row", "col", None, None),
        check_vma=False,
    )
```
